32 devices in a mesh: col: 8 (over z, x), row: 4 (over y, core).
Axes of the slice: x: 2, y: 2, z: 4, core: 2. Of those that a mesh axis runs over, the one named last changes fastest.
Arguments:
- right_side: float32 [8, 256, 256], P('col'), may hold values from -6 to 6
- coupling: bfloat16 [2, 4, 256, 81920], P(None, 'row', None, 'col'), may hold values from -0.01953125 to 0.01953125
- child_solution: bfloat16 [81920, 256], P(('col', 'row')), may hold values from -6 to 6
- factor_blocks: bfloat16 [2, 4, 256, 8, 256], P(None, 'row', None, 'col'), may hold values from -1 to 1
- pattern: int32 [8, 8], replicated, may hold values from 0 to 1, as said below
- diag_inverse: bfloat16 [8, 256, 256], P('col'), may hold values from -0.375 to 0.375
Outputs:
- solved: bfloat16 [8, 256, 256], P('col')
The draws below stay inside these ranges and needn't reach their ends.
Inputs may be any that keep to these rules, and one draw needn't show every extreme that they name: pattern[j, j - 1] = 1 for every j from 1 to 7; entries with k >= j are not read.
All inputs are finite; a program needn't handle non-finite values.
Results may differ from the reference program's by a relative error of at most 0.017.
Values may be sent and summed in bfloat16 or wider, within the bound.
A program may use at most 64 MiB of HBM per device.

```python
import math
import jax
import jax.numpy as jnp
from jax import lax

BS = 256
RHS = 256
NB = 8
CG = 1
BSG = 256
BR = 2
KW = 81920
N_COL = 8
N_ROW = 4


def draw_pattern(key, part):
    coins = jax.random.randint(key, (NB, NB), 0, 4)
    base = (coins < 3).astype(jnp.int32)
    rows = jnp.arange(NB, dtype=jnp.int32)[:, None]
    cols = jnp.arange(NB, dtype=jnp.int32)[None, :]
    return jnp.where(rows == cols + 1, jnp.int32(1), base)


def draw_factor_blocks(key, part):
    shape = (BR, N_ROW, BS, N_COL, BSG)
    values = jax.random.truncated_normal(key, -4.0, 4.0, shape, jnp.float32)
    outer = jnp.arange(BR, dtype=jnp.int32)[:, None, None, None, None]
    inner = jnp.arange(N_ROW, dtype=jnp.int32)[None, :, None, None, None]
    block_row = outer * N_ROW + inner
    block_col = (jnp.arange(N_COL, dtype=jnp.int32) // CG)[None, None, None, :, None]
    chain = block_row == block_col + 1
    strong = jnp.float32(0.9 / math.sqrt(BS))
    weak = jnp.float32(1.0 / math.sqrt(BS * NB))
    scale = jnp.where(chain, strong, weak)
    return (values * scale).astype(jnp.bfloat16)


def steps_of(own_key, extent, split, smallest, largest):
    level, own = 1.0, jax.random.fold_in(own_key, 6)
    for position, parts in split:
        heights = jnp.exp(jax.random.uniform(jax.random.fold_in(own, position), (parts,), jnp.float32, smallest / len(split), largest / len(split)))
        level = level * jnp.repeat(heights, extent[position] // parts).reshape([-1 if axis == position else 1 for axis in range(len(extent))])
    return level


def gaussian(rng, extent, spread, limit, cuts=(), kind=jnp.bfloat16):
    gain = steps_of(rng, extent, cuts, -0.22, 0.18) if cuts else 1.0
    drawn = jax.random.normal(rng, extent, jnp.float32) * spread * gain
    return jnp.minimum(jnp.maximum(drawn, -limit), limit).astype(kind)


def setup_inputs(seed: int = 0) -> dict:
    key_of = jax.random.split(jax.random.key(seed), 7)
    return {
        "right_side": gaussian(key_of[0], (N_COL, BSG, RHS), 1.0, 6.0, ((0, 8),), jnp.float32),
        "coupling": gaussian(key_of[1], (BR, N_ROW, BS, KW), KW ** -0.5, 0.01953125, ((1, 4), (3, 8))),
        "child_solution": gaussian(key_of[2], (KW, RHS), 1.0, 6.0, ((0, 32),)),
        "factor_blocks": draw_factor_blocks(jax.random.fold_in(key_of[6], 71), 0),
        "pattern": draw_pattern(jax.random.fold_in(key_of[6], 71), 0),
        "diag_inverse": gaussian(key_of[5], (N_COL, BSG, BS), BS ** -0.5, 0.375, ((0, 8),)),
    }


def reference(right_side, coupling, child_solution, factor_blocks, pattern, diag_inverse):
    coupled = coupling.reshape(NB, BS, KW)
    update = lax.map(lambda blk: jnp.dot(blk, child_solution, preferred_element_type=jnp.float32), coupled)
    blocks = factor_blocks.reshape(NB, BS, NB * BS)
    inverse = diag_inverse.reshape(NB, BS, BS)
    rhs = right_side.reshape(NB, BS, RHS)
    positions = jnp.arange(NB, dtype=jnp.int32)
    solved = jnp.zeros((NB, BS, RHS), jnp.bfloat16)
    for j in range(NB):
        keep = (pattern[j] > 0) & (positions < j)
        masked = jnp.where(keep[:, None, None], solved, jnp.zeros_like(solved))
        sub_j = jnp.dot(blocks[j], masked.reshape(NB * BS, RHS), preferred_element_type=jnp.float32)
        rest = (rhs[j] - update[j] - sub_j).astype(jnp.bfloat16)
        fresh = jnp.dot(inverse[j], rest, preferred_element_type=jnp.float32).astype(jnp.bfloat16)
        solved = solved.at[j].set(fresh)
    return solved.reshape(N_COL, BS // (N_COL // NB), RHS)
```

```python
import functools

import jax
import jax.numpy as jnp
from jax import lax
from jax.experimental import pallas as pl
from jax.experimental.pallas import tpu as pltpu
from jax.sharding import PartitionSpec as P

MESH = pl.DeviceIdType.MESH
BF16 = jnp.bfloat16
F32 = jnp.float32


def dot(a, b):
    return jnp.dot(a, b, preferred_element_type=F32)


def kernel(
    nch, rhs_ref, cpl_hbm, child_hbm, fac_hbm, pat_ref, dinv_ref, out_ref,
    cpl, gath, acc, fac, part, precv, diag, rside, rest, sol,
    loc_sem, m_sem, y_send, y_recv, f_send, f_recv, fac_send, fac_recv,
    d_sem, p_send, p_recv, ch_send, ch_recv, o_send, o_recv,
):
    nrow = lax.axis_size("row")
    ncol = lax.axis_size("col")
    nslab = ncol // 2
    r = lax.axis_index("row")
    c = lax.axis_index("col")
    y, core = r // 2, r % 2
    z, x = c // 2, c % 2
    mate = 2 * y + 1 - core
    across = 2 * (1 - y) + core
    mate_across = 2 * (1 - y) + 1 - core
    depth = child_hbm.shape[0]
    step = depth // nch
    half = rhs_ref.shape[2] // 2
    solver = (core == 0) & (z % 2 == y)

    def remote(src, dst, ss, rs, row, col):
        return pltpu.make_async_remote_copy(
            src_ref=src, dst_ref=dst, send_sem=ss, recv_sem=rs,
            device_id={"row": row, "col": col}, device_id_type=MESH,
        )

    own = pltpu.make_async_copy(child_hbm, gath.at[r], loc_sem.at[0])
    load = pltpu.make_async_copy(cpl_hbm, cpl, loc_sem.at[1])
    own.start()
    load.start()

    barrier = pltpu.get_barrier_semaphore()
    for dr in range(nrow):
        for dc in range(ncol):
            if dr or dc:
                pl.semaphore_signal(
                    barrier, inc=1,
                    device_id={"row": (r + dr) % nrow, "col": (c + dc) % ncol},
                    device_id_type=MESH,
                )
    pl.semaphore_wait(barrier, nrow * ncol - 1)

    def rows(i):
        return pl.ds(pl.multiple_of(i * step, step), step)

    def y_copy(i):
        return remote(child_hbm.at[rows(i)], gath.at[r, rows(i)], y_send.at[i], y_recv.at[i], across, c)

    def y_arrival(i):
        return remote(child_hbm.at[rows(i)], gath.at[across, rows(i)], y_send.at[i], y_recv.at[i], across, c)

    def forward(i):
        return remote(gath.at[across, rows(i)], gath.at[across, rows(i)], f_send.at[i], f_recv.at[i], mate, c)

    def f_arrival(i):
        return remote(
            gath.at[mate_across, rows(i)], gath.at[mate_across, rows(i)], f_send.at[i], f_recv.at[i], mate, c)

    for i in range(nch):
        y_copy(i).start()
    m_copy = remote(child_hbm, gath.at[r], m_sem.at[0], m_sem.at[1], mate, c)
    m_copy.start()

    def fac_copy(s, xd):
        return remote(
            fac_hbm.at[s], fac.at[core, c], fac_send.at[s, xd], fac_recv.at[core, c],
            2 * y, 2 * (y + 2 * s) + xd)

    for s in range(2):
        @pl.when(c < r + nrow * s)
        def _():
            for xd in range(2):
                fac_copy(s, xd).start()

    d_copy = remote(dinv_ref.at[0], diag.at[x], d_sem.at[0], d_sem.at[1], r, c + 1 - 2 * x)
    other_cols = pl.ds(pl.multiple_of((1 - x) * half, half), half)
    my_cols = pl.ds(pl.multiple_of(x * half, half), half)
    r_copy = remote(rhs_ref.at[0, :, other_cols], rside.at[x], d_sem.at[2], d_sem.at[3], r, c + 1 - 2 * x)

    @pl.when(solver)
    def _():
        d_copy.start()
        r_copy.start()
        diag[x] = dinv_ref[0]
        rside[x] = rhs_ref[0, :, my_cols]

    acc[...] = jnp.zeros_like(acc)

    def piece(slot, i):
        cols = pl.ds(pl.multiple_of(slot * depth + i * step, step), step)
        block = gath[slot, rows(i)]
        for b in range(2):
            acc[b] += dot(cpl[b, :, cols], block)

    own.wait()
    load.wait()

    @pl.loop(0, nch)
    def _(i):
        piece(r, i)

    remote(child_hbm, gath.at[mate], m_sem.at[0], m_sem.at[1], mate, c).wait_recv()

    @pl.loop(0, nch)
    def _(i):
        piece(mate, i)

    @pl.loop(0, nch)
    def _(i):
        y_arrival(i).wait_recv()
        forward(i).start()
        piece(across, i)
        f_arrival(i).wait_recv()
        piece(mate_across, i)

    def p_copy(s, xd):
        return remote(
            part.at[s, xd], precv.at[core, c], p_send.at[s, xd], p_recv.at[core, c],
            2 * y, 2 * (y + 2 * s) + xd)

    def p_self(s, xd):
        return solver & (c == 2 * (y + 2 * s) + xd)

    for s in range(2):
        for xd in range(2):
            part[s, xd] = acc[s, :, xd * half:(xd + 1) * half].astype(BF16)

            @pl.when(jnp.logical_not(p_self(s, xd)))
            def _():
                p_copy(s, xd).start()

    def chain_copy(zd):
        return remote(
            sol.at[z], sol.at[z], ch_send.at[zd], ch_recv.at[z], 2 * (zd % 2), 2 * zd + x)

    def out_copy(xo, ro):
        return remote(
            sol.at[z, xo], out_ref.at[0, :, my_cols], o_send.at[xo, ro], o_recv.at[x], ro, 2 * z + xo)

    def out_self(xo, ro):
        return (r == ro) & (x == xo)

    @pl.when(solver)
    def _():
        mine = acc[z // 2, :, my_cols]
        d_copy.wait_recv()
        r_copy.wait_recv()
        rest[0] = rside[0] - mine
        rest[1] = rside[1]
        for p in range(2):
            for k in range(ncol):
                slot = precv.at[p, k]

                def take():
                    remote(slot, slot, p_send.at[0, 0], p_recv.at[p, k], r, c).wait_recv()
                    rest[p] = rest[p] - slot[...].astype(F32)

                if p == 0:
                    pl.when(c != k)(take)
                else:
                    take()
        for p in range(2):
            for k in range(ncol):
                @pl.when(k < 2 * z + p)
                def _():
                    remote(
                        fac.at[p, k], fac.at[p, k], fac_send.at[0, 0], fac_recv.at[p, k], r, c).wait_recv()

        def term(p, k, value):
            flag = jnp.where(pat_ref[2 * z + p, k] > 0, 1.0, 0.0).astype(F32)
            rest[p] = rest[p] - flag * dot(fac[p, k], value)

        for zz in range(nslab - 1):
            @pl.when(zz < z)
            def _():
                remote(sol.at[zz], sol.at[zz], ch_send.at[0], ch_recv.at[zz], r, c).wait_recv()
                for q in range(2):
                    for p in range(2):
                        term(p, 2 * zz + q, sol[zz, q])

        first = dot(diag[0], rest[0].astype(BF16)).astype(BF16)
        sol[z, 0] = first
        term(1, 2 * z, first)
        sol[z, 1] = dot(diag[1], rest[1].astype(BF16)).astype(BF16)
        for zd in range(1, nslab):
            @pl.when(zd > z)
            def _():
                chain_copy(zd).start()
        for xo in range(2):
            for ro in range(nrow):
                @pl.when(jnp.logical_not(out_self(xo, ro)))
                def _():
                    out_copy(xo, ro).start()
        out_ref[0, :, my_cols] = sol[z, x]

    for xs in range(2):
        @pl.when(jnp.logical_not(solver & (x == xs)))
        def _():
            spot = out_ref.at[0, :, pl.ds(xs * half, half)]
            remote(sol.at[0, 0], spot, o_send.at[0, 0], o_recv.at[xs], r, c).wait_recv()

    m_copy.wait_send()

    @pl.loop(0, nch)
    def _(i):
        y_copy(i).wait_send()
        forward(i).wait_send()

    for s in range(2):
        @pl.when(c < r + nrow * s)
        def _():
            for xd in range(2):
                fac_copy(s, xd).wait_send()

        for xd in range(2):
            @pl.when(jnp.logical_not(p_self(s, xd)))
            def _():
                p_copy(s, xd).wait_send()

    @pl.when(solver)
    def _():
        d_copy.wait_send()
        r_copy.wait_send()
        for zd in range(1, nslab):
            @pl.when(zd > z)
            def _():
                chain_copy(zd).wait_send()
        for xo in range(2):
            for ro in range(nrow):
                @pl.when(jnp.logical_not(out_self(xo, ro)))
                def _():
                    out_copy(xo, ro).wait_send()


def fused(right_side, coupling, child_solution, factor_blocks, pattern, diag_inverse):
    nrow = lax.axis_size("row")
    ncol = lax.axis_size("col")
    brows, _, bs, kcols = coupling.shape
    depth, rhs = child_solution.shape
    nch = depth // 256
    half = rhs // 2
    dma = pltpu.SemaphoreType.DMA
    hbm = pl.BlockSpec(memory_space=pltpu.HBM)
    vmem = pl.BlockSpec(memory_space=pltpu.VMEM)
    flops = 2 * brows * bs * kcols * rhs
    return pl.pallas_call(
        functools.partial(kernel, nch),
        out_shape=jax.ShapeDtypeStruct((1, bs, rhs), BF16),
        in_specs=[vmem, hbm, hbm, hbm, pl.BlockSpec(memory_space=pltpu.SMEM), vmem],
        out_specs=vmem,
        scratch_shapes=[
            pltpu.VMEM((brows, bs, kcols), BF16),
            pltpu.VMEM((nrow, depth, rhs), BF16),
            pltpu.VMEM((brows, bs, rhs), F32),
            pltpu.VMEM((2, ncol, bs, bs), BF16),
            pltpu.VMEM((2, 2, bs, half), BF16),
            pltpu.VMEM((2, ncol, bs, half), BF16),
            pltpu.VMEM((2, bs, bs), BF16),
            pltpu.VMEM((2, bs, half), F32),
            pltpu.VMEM((2, bs, half), F32),
            pltpu.VMEM((ncol // 2, 2, bs, half), BF16),
            dma((2,)), dma((2,)), dma((nch,)), dma((nch,)), dma((nch,)), dma((nch,)),
            dma((2, 2)), dma((2, ncol)), dma((4,)), dma((2, 2)), dma((2, ncol)),
            dma((ncol // 2,)), dma((ncol // 2,)), dma((2, nrow)), dma((2,)),
        ],
        compiler_params=pltpu.CompilerParams(
            collective_id=0, has_side_effects=True, vmem_limit_bytes=48 * 1024 * 1024
        ),
        cost_estimate=pl.CostEstimate(
            flops=flops, bytes_accessed=2 * brows * bs * kcols, transcendentals=0),
    )(
        right_side,
        coupling.reshape(brows, bs, kcols),
        child_solution,
        factor_blocks.reshape(brows, bs, bs),
        pattern,
        diag_inverse,
    )


def general(right_side, coupling, child_solution, factor_blocks, pattern, diag_inverse):
    nrow = lax.axis_size("row")
    ncol = lax.axis_size("col")
    row_index = lax.axis_index("row")
    col_index = lax.axis_index("col")
    brows = coupling.shape[0]
    blk_size = coupling.shape[2]
    kcols = coupling.shape[3]
    rhs_count = child_solution.shape[1]
    nblk = pattern.shape[0]
    group = ncol // nblk
    part_rows = blk_size // group
    my_block = col_index // group
    my_offset = col_index % group * part_rows
    flat = coupling.reshape(brows * blk_size, kcols)
    update = jnp.dot(
        flat,
        lax.all_gather(child_solution, "row", axis=0, tiled=True),
        preferred_element_type=jnp.float32,
    )
    update = update.reshape(brows, blk_size, rhs_count)
    rhs_part = right_side.reshape(part_rows, rhs_count)
    placed = lax.dynamic_update_slice(
        jnp.zeros((blk_size, rhs_count), jnp.float32), rhs_part, (my_offset, jnp.int32(0))
    )
    blocks = factor_blocks.reshape(brows, blk_size, part_rows)
    inv_rows = diag_inverse.reshape(part_rows, blk_size)

    def advance(j, solved):
        j_row = j % nrow
        j_arow = j // nrow
        flags = lax.dynamic_index_in_dim(pattern, j, 0, keepdims=False)
        flag = lax.dynamic_index_in_dim(flags, my_block, 0, keepdims=False)
        keep = (flag > 0) & (my_block < j)
        masked = jnp.where(keep, solved, jnp.zeros_like(solved))
        row_blocks = lax.dynamic_index_in_dim(blocks, j_arow, 0, keepdims=False)
        partial_value = jnp.dot(row_blocks, masked, preferred_element_type=jnp.float32)
        partial_value = partial_value + lax.dynamic_index_in_dim(update, j_arow, 0, keepdims=False)
        partial_value = jnp.where(my_block == j, placed, jnp.zeros_like(placed)) - partial_value
        partial_value = jnp.where(row_index == j_row, partial_value, jnp.zeros_like(partial_value))
        total = lax.psum(partial_value, ("col", "row"))
        fresh = jnp.dot(
            inv_rows, total.astype(jnp.bfloat16), preferred_element_type=jnp.float32
        ).astype(jnp.bfloat16)
        return jnp.where(my_block == j, fresh, solved)

    start_state = jnp.zeros((part_rows, rhs_count), jnp.bfloat16)
    solved = lax.fori_loop(0, nblk, advance, start_state)
    return solved.reshape(1, part_rows, rhs_count)


def solution(mesh):
    nrow, ncol = mesh.shape["row"], mesh.shape["col"]
    in_specs = (
        P("col", None, None),
        P(None, "row", None, "col"),
        P(("col", "row"), None),
        P(None, "row", None, "col", None),
        P(),
        P("col", None, None),
    )

    def per_device(right_side, coupling, child_solution, factor_blocks, pattern, diag_inverse):
        paired = nrow == 4 and ncol == 8 and pattern.shape[0] == 8
        body = fused if paired else general
        return body(right_side, coupling, child_solution, factor_blocks, pattern, diag_inverse)

    return jax.shard_map(
        per_device, mesh=mesh, in_specs=in_specs, out_specs=P("col", None, None), check_vma=False
    )
```

```python
import functools

import jax
import jax.numpy as jnp
from jax import lax
from jax.experimental import pallas as pl
from jax.experimental.pallas import tpu as pltpu
from jax.sharding import PartitionSpec as P

MESH = pl.DeviceIdType.MESH
BF16 = jnp.bfloat16
F32 = jnp.float32


def dot(a, b):
    return jnp.dot(a, b, preferred_element_type=F32)


def kernel(
    nch, rhs_hbm, cpl_hbm, child_hbm, fac_hbm, pat_hbm, dinv_hbm, out_ref,
    pat_ref, cpl, gath, acc, fac, xpart, xrecv, part, precv, diag, rside, below, gain, rest, sol,
    loc_sem, m_send, m_recv, y_send, y_recv, f_send, f_recv, fac_send, fac_recv,
    d_sem, x_sem, p_send, p_recv, ch_send, ch_recv, o_send, o_recv,
):
    nrow = lax.axis_size("row")
    ncol = lax.axis_size("col")
    nslab = ncol // 2
    r = lax.axis_index("row")
    c = lax.axis_index("col")
    y, core = r // 2, r % 2
    z, x = c // 2, c % 2
    mate = 2 * y + 1 - core
    across = 2 * (1 - y) + core
    mate_across = 2 * (1 - y) + 1 - core
    beside = c + 1 - 2 * x
    depth = child_hbm.shape[0]
    step = depth // nch
    half = rhs_hbm.shape[2] // 2
    solver = (core == 0) & (z % 2 == y)
    other_cols = pl.ds(pl.multiple_of((1 - x) * half, half), half)
    my_cols = pl.ds(pl.multiple_of(x * half, half), half)
    halves = (other_cols, my_cols)

    def remote(src, dst, ss, rs, row, col):
        return pltpu.make_async_remote_copy(
            src_ref=src, dst_ref=dst, send_sem=ss, recv_sem=rs,
            device_id={"row": row, "col": col}, device_id_type=MESH,
        )

    def arrival(ref, sem):
        return remote(ref, ref, d_sem.at[0], sem, mate, c)

    own = [
        pltpu.make_async_copy(child_hbm.at[:, halves[h]], gath.at[h, r], loc_sem.at[h])
        for h in range(2)
    ]
    load = pltpu.make_async_copy(cpl_hbm, cpl, loc_sem.at[2])
    flags = pltpu.make_async_copy(pat_hbm, pat_ref, loc_sem.at[3])
    d_own = pltpu.make_async_copy(dinv_hbm.at[0], diag.at[x], loc_sem.at[4])
    r_own = pltpu.make_async_copy(rhs_hbm.at[0, :, my_cols], rside.at[x], loc_sem.at[5])
    for copy in (own[0], own[1], load, flags, d_own, r_own):
        copy.start()

    barrier = pltpu.get_barrier_semaphore()
    for dr in range(nrow):
        for dc in range(ncol):
            if dr or dc:
                pl.semaphore_signal(
                    barrier, inc=1,
                    device_id={"row": (r + dr) % nrow, "col": (c + dc) % ncol},
                    device_id_type=MESH,
                )
    pl.semaphore_wait(barrier, nrow * ncol - 1)

    def rows(i):
        return pl.ds(pl.multiple_of(i * step, step), step)

    def y_copy(h, i):
        return remote(
            child_hbm.at[rows(i), halves[h]], gath.at[h, r, rows(i)],
            y_send.at[h, i], y_recv.at[h, i], across, c)

    def forward(h, i):
        spot = gath.at[h, across, rows(i)]
        return remote(spot, spot, f_send.at[h, i], f_recv.at[h, i], mate, c)

    def m_copy(h):
        return remote(
            child_hbm.at[:, halves[h]], gath.at[h, r], m_send.at[h], m_recv.at[h], mate, c)

    for i in range(nch):
        y_copy(0, i).start()
    for h in range(2):
        m_copy(h).start()

    def fac_copy(s, xd):
        return remote(
            fac_hbm.at[s], fac.at[core, c], fac_send.at[s, xd], fac_recv.at[core, c],
            2 * y, 2 * (y + 2 * s) + xd)

    for s in range(2):
        @pl.when(c < r + nrow * s)
        def _():
            for xd in range(2):
                fac_copy(s, xd).start()

    d_copy = remote(dinv_hbm.at[0], diag.at[x], d_sem.at[0], d_sem.at[1], r, beside)
    r_copy = remote(rhs_hbm.at[0, :, other_cols], rside.at[x], d_sem.at[2], d_sem.at[3], r, beside)

    @pl.when(solver)
    def _():
        d_copy.start()
        r_copy.start()

    acc[...] = jnp.zeros_like(acc)

    def piece(h, slot, i):
        cols = pl.ds(pl.multiple_of(slot * depth + i * step, step), step)
        block = gath[h, slot, rows(i)]
        for b in range(2):
            acc[h, b] += dot(cpl[b, :, cols], block)

    def flag(p, k):
        return jnp.where(pat_ref[2 * z + p, k] > 0, 1.0, 0.0).astype(F32)

    def prepare():
        d_own.wait()
        r_own.wait()
        arrival(diag.at[1 - x], d_sem.at[1]).wait_recv()
        arrival(rside.at[1 - x], d_sem.at[3]).wait_recv()
        for p in range(2):
            for k in range(ncol - 1):
                @pl.when(k < 2 * z + p)
                def _():
                    arrival(fac.at[p, k], fac_recv.at[p, k]).wait_recv()
        inner = flag(1, 2 * z) * dot(fac[1, 2 * z], diag[0])
        below[...] = -dot(diag[1], inner.astype(BF16)).astype(BF16)
        for zz in range(nslab - 1):
            @pl.when(zz < z)
            def _():
                @pl.loop(0, 2)
                def _(q):
                    k = 2 * zz + q
                    gain[zz, q, 0] = (flag(0, k) * dot(diag[0], fac[0, k])).astype(BF16)
                    gain[zz, q, 1] = (
                        flag(1, k) * dot(diag[1], fac[1, k]) + flag(0, k) * dot(below[...], fac[0, k])
                    ).astype(BF16)

    flags.wait()
    load.wait()
    for h in range(2):
        own[h].wait()

        @pl.loop(0, nch)
        def _(i):
            piece(h, r, i)

        arrival(gath.at[h, mate], m_recv.at[h]).wait_recv()

        @pl.loop(0, nch)
        def _(i):
            piece(h, mate, i)

        if h == 1:
            continue

        @pl.loop(0, nch)
        def _(i):
            arrival(gath.at[0, across, rows(i)], y_recv.at[0, i]).wait_recv()
            y_copy(1, i).start()
            forward(0, i).start()
            piece(0, across, i)
            arrival(gath.at[0, mate_across, rows(i)], f_recv.at[0, i]).wait_recv()
            piece(0, mate_across, i)

        xpart[...] = acc[0].astype(BF16)
        x_copy = remote(xpart, xrecv, x_sem.at[0], x_sem.at[1], r, beside)
        x_copy.start()
        pl.when(solver)(prepare)

    @pl.loop(0, nch)
    def _(i):
        arrival(gath.at[1, across, rows(i)], y_recv.at[1, i]).wait_recv()
        forward(1, i).start()
        piece(1, across, i)
        arrival(gath.at[1, mate_across, rows(i)], f_recv.at[1, i]).wait_recv()
        piece(1, mate_across, i)

    x_copy.wait_recv()

    def p_copy(s):
        return remote(
            part.at[s], precv.at[core, z], p_send.at[s], p_recv.at[core, z],
            2 * y, 2 * (y + 2 * s) + x)

    def p_self(s):
        return solver & (z == y + 2 * s)

    for s in range(2):
        acc[1, s] = acc[1, s] + xrecv[s].astype(F32)
        part[s] = acc[1, s].astype(BF16)

        @pl.when(jnp.logical_not(p_self(s)))
        def _():
            p_copy(s).start()

    def chain_copy(zd):
        return remote(
            sol.at[z], sol.at[z], ch_send.at[zd], ch_recv.at[z], 2 * (zd % 2), 2 * zd + x)

    def out_copy(xo, ro):
        return remote(
            sol.at[z, xo], out_ref.at[0, :, my_cols], o_send.at[xo, ro], o_recv.at[x], ro, 2 * z + xo)

    def out_self(xo, ro):
        return (r == ro) & (x == xo)

    def send_out(xo):
        for ro in range(nrow):
            @pl.when(jnp.logical_not(out_self(xo, ro)))
            def _():
                out_copy(xo, ro).start()

    @pl.when(jnp.logical_not(solver))
    def _():
        d_own.wait()
        r_own.wait()

    @pl.when(solver)
    def _():
        rest[0] = rside[0] - acc[1, z // 2]
        rest[1] = rside[1]
        for p in range(2):
            for k in range(nslab):
                def take():
                    arrival(precv.at[p, k], p_recv.at[p, k]).wait_recv()
                    rest[p] = rest[p] - precv[p, k].astype(F32)

                if p == 0:
                    pl.when(z != k)(take)
                else:
                    take()

        upper = rest[0].astype(BF16)
        lower = rest[1].astype(BF16)
        rest[0] = dot(diag[0], upper)
        rest[1] = dot(diag[1], lower) + dot(below[...], upper)
        for zz in range(nslab - 1):
            @pl.when(zz < z)
            def _():
                arrival(sol.at[zz], ch_recv.at[zz]).wait_recv()
                for p in range(2):
                    rest[p] = rest[p] - (dot(gain[zz, 0, p], sol[zz, 0]) + dot(gain[zz, 1, p], sol[zz, 1]))

        sol[z] = rest[...].astype(BF16)
        for zd in range(1, nslab):
            @pl.when(zd == z + 1)
            def _():
                chain_copy(zd).start()
                chain_copy(zd).wait_send()
        for zd in range(2, nslab):
            @pl.when(zd > z + 1)
            def _():
                chain_copy(zd).start()
        send_out(0)
        send_out(1)
        out_ref[0, :, my_cols] = sol[z, x]

    m_copy(0).wait_send()
    m_copy(1).wait_send()
    x_copy.wait_send()
    for h in range(2):
        @pl.loop(0, nch)
        def _(i):
            y_copy(h, i).wait_send()
            forward(h, i).wait_send()

    for s in range(2):
        @pl.when(c < r + nrow * s)
        def _():
            for xd in range(2):
                fac_copy(s, xd).wait_send()

        @pl.when(jnp.logical_not(p_self(s)))
        def _():
            p_copy(s).wait_send()

    for xs in range(2):
        @pl.when(jnp.logical_not(solver & (x == xs)))
        def _():
            arrival(out_ref.at[0, :, pl.ds(xs * half, half)], o_recv.at[xs]).wait_recv()

    @pl.when(solver)
    def _():
        d_copy.wait_send()
        r_copy.wait_send()
        for zd in range(2, nslab):
            @pl.when(zd > z + 1)
            def _():
                chain_copy(zd).wait_send()
        for xo in range(2):
            for ro in range(nrow):
                @pl.when(jnp.logical_not(out_self(xo, ro)))
                def _():
                    out_copy(xo, ro).wait_send()


def fused(right_side, coupling, child_solution, factor_blocks, pattern, diag_inverse):
    nrow = lax.axis_size("row")
    ncol = lax.axis_size("col")
    brows, _, bs, kcols = coupling.shape
    depth, rhs = child_solution.shape
    nch = depth // 512
    half = rhs // 2
    dma = pltpu.SemaphoreType.DMA
    hbm = pl.BlockSpec(memory_space=pltpu.HBM)
    vmem = pl.BlockSpec(memory_space=pltpu.VMEM)
    flops = 2 * brows * bs * kcols * rhs
    return pl.pallas_call(
        functools.partial(kernel, nch),
        out_shape=jax.ShapeDtypeStruct((1, bs, rhs), BF16),
        in_specs=[hbm] * 6,
        out_specs=vmem,
        scratch_shapes=[
            pltpu.SMEM(pattern.shape, pattern.dtype),
            pltpu.VMEM((brows, bs, kcols), BF16),
            pltpu.VMEM((2, nrow, depth, half), BF16),
            pltpu.VMEM((2, brows, bs, half), F32),
            pltpu.VMEM((2, ncol, bs, bs), BF16),
            pltpu.VMEM((brows, bs, half), BF16),
            pltpu.VMEM((brows, bs, half), BF16),
            pltpu.VMEM((brows, bs, half), BF16),
            pltpu.VMEM((2, ncol // 2, bs, half), BF16),
            pltpu.VMEM((2, bs, bs), BF16),
            pltpu.VMEM((2, bs, half), F32),
            pltpu.VMEM((bs, bs), BF16),
            pltpu.VMEM((ncol // 2 - 1, 2, 2, bs, bs), BF16),
            pltpu.VMEM((2, bs, half), F32),
            pltpu.VMEM((ncol // 2, 2, bs, half), BF16),
            dma((6,)), dma((2,)), dma((2,)),
            dma((2, nch)), dma((2, nch)), dma((2, nch)), dma((2, nch)),
            dma((2, 2)), dma((2, ncol)), dma((4,)), dma((2,)), dma((2,)), dma((2, ncol // 2)),
            dma((ncol // 2,)), dma((ncol // 2,)), dma((2, nrow)), dma((2,)),
        ],
        compiler_params=pltpu.CompilerParams(
            collective_id=0, has_side_effects=True, vmem_limit_bytes=62 * 1024 * 1024
        ),
        cost_estimate=pl.CostEstimate(
            flops=flops, bytes_accessed=2 * brows * bs * kcols, transcendentals=0),
    )(
        right_side,
        coupling.reshape(brows, bs, kcols),
        child_solution,
        factor_blocks.reshape(brows, bs, bs),
        pattern,
        diag_inverse,
    )


def general(right_side, coupling, child_solution, factor_blocks, pattern, diag_inverse):
    nrow = lax.axis_size("row")
    ncol = lax.axis_size("col")
    row_index = lax.axis_index("row")
    col_index = lax.axis_index("col")
    brows = coupling.shape[0]
    blk_size = coupling.shape[2]
    kcols = coupling.shape[3]
    rhs_count = child_solution.shape[1]
    nblk = pattern.shape[0]
    group = ncol // nblk
    part_rows = blk_size // group
    my_block = col_index // group
    my_offset = col_index % group * part_rows
    flat = coupling.reshape(brows * blk_size, kcols)
    update = jnp.dot(
        flat,
        lax.all_gather(child_solution, "row", axis=0, tiled=True),
        preferred_element_type=jnp.float32,
    )
    update = update.reshape(brows, blk_size, rhs_count)
    rhs_part = right_side.reshape(part_rows, rhs_count)
    placed = lax.dynamic_update_slice(
        jnp.zeros((blk_size, rhs_count), jnp.float32), rhs_part, (my_offset, jnp.int32(0))
    )
    blocks = factor_blocks.reshape(brows, blk_size, part_rows)
    inv_rows = diag_inverse.reshape(part_rows, blk_size)

    def advance(j, solved):
        j_row = j % nrow
        j_arow = j // nrow
        flags = lax.dynamic_index_in_dim(pattern, j, 0, keepdims=False)
        flag = lax.dynamic_index_in_dim(flags, my_block, 0, keepdims=False)
        keep = (flag > 0) & (my_block < j)
        masked = jnp.where(keep, solved, jnp.zeros_like(solved))
        row_blocks = lax.dynamic_index_in_dim(blocks, j_arow, 0, keepdims=False)
        partial_value = jnp.dot(row_blocks, masked, preferred_element_type=jnp.float32)
        partial_value = partial_value + lax.dynamic_index_in_dim(update, j_arow, 0, keepdims=False)
        partial_value = jnp.where(my_block == j, placed, jnp.zeros_like(placed)) - partial_value
        partial_value = jnp.where(row_index == j_row, partial_value, jnp.zeros_like(partial_value))
        total = lax.psum(partial_value, ("col", "row"))
        fresh = jnp.dot(
            inv_rows, total.astype(jnp.bfloat16), preferred_element_type=jnp.float32
        ).astype(jnp.bfloat16)
        return jnp.where(my_block == j, fresh, solved)

    start_state = jnp.zeros((part_rows, rhs_count), jnp.bfloat16)
    solved = lax.fori_loop(0, nblk, advance, start_state)
    return solved.reshape(1, part_rows, rhs_count)


def solution(mesh):
    nrow, ncol = mesh.shape["row"], mesh.shape["col"]
    in_specs = (
        P("col", None, None),
        P(None, "row", None, "col"),
        P(("col", "row"), None),
        P(None, "row", None, "col", None),
        P(),
        P("col", None, None),
    )

    def per_device(right_side, coupling, child_solution, factor_blocks, pattern, diag_inverse):
        paired = nrow == 4 and ncol == 8 and pattern.shape[0] == 8
        body = fused if paired else general
        return body(right_side, coupling, child_solution, factor_blocks, pattern, diag_inverse)

    return jax.shard_map(
        per_device, mesh=mesh, in_specs=in_specs, out_specs=P("col", None, None), check_vma=False
    )
```

```python
import functools

import jax
import jax.numpy as jnp
from jax import lax
from jax.experimental import pallas as pl
from jax.experimental.pallas import tpu as pltpu
from jax.sharding import PartitionSpec as P

MESH = pl.DeviceIdType.MESH
BF16 = jnp.bfloat16
F32 = jnp.float32


def dot(a, b):
    return jnp.dot(a, b, preferred_element_type=F32)


def kernel(
    nch, rhs_hbm, cpl_hbm, child_hbm, fac_hbm, pat_hbm, dinv_hbm, out_ref,
    pat_ref, cpl, gath, acc, fac, xpart, xrecv, part, precv, diag, rside, below, gain, rest, sol,
    loc_sem, m_send, m_recv, y_send, y_recv, f_send, f_recv, fac_send, fac_recv,
    d_send, d_recv, r_send, r_recv, x_sem, p_send, p_recv, ch_send, ch_recv, o_send, o_recv, g_send,
):
    nrow = lax.axis_size("row")
    ncol = lax.axis_size("col")
    nslab = ncol // 2
    r = lax.axis_index("row")
    c = lax.axis_index("col")
    y, core = r // 2, r % 2
    z, x = c // 2, c % 2
    mate = 2 * y + 1 - core
    across = 2 * (1 - y) + core
    mate_across = 2 * (1 - y) + 1 - core
    beside = c + 1 - 2 * x
    depth = child_hbm.shape[0]
    step = depth // nch
    half = rhs_hbm.shape[2] // 2
    home = (core == 0) & (z % 2 == y)
    solver = (core == 0) & (z >= 1) & (z <= nslab // 2)
    slab = 2 * (z - 1) + y
    other_cols = pl.ds(pl.multiple_of((1 - x) * half, half), half)
    my_cols = pl.ds(pl.multiple_of(x * half, half), half)
    halves = (other_cols, my_cols)

    def remote(src, dst, ss, rs, row, col):
        return pltpu.make_async_remote_copy(
            src_ref=src, dst_ref=dst, send_sem=ss, recv_sem=rs,
            device_id={"row": row, "col": col}, device_id_type=MESH,
        )

    def arrival(ref, sem):
        return remote(ref, ref, d_send.at[0], sem, mate, c)

    own = [
        pltpu.make_async_copy(child_hbm.at[:, halves[h]], gath.at[h, r], loc_sem.at[h])
        for h in range(2)
    ]
    load = pltpu.make_async_copy(cpl_hbm, cpl, loc_sem.at[2])
    flags = pltpu.make_async_copy(pat_hbm, pat_ref, loc_sem.at[3])
    for copy in (own[0], own[1], load, flags):
        copy.start()

    barrier = pltpu.get_barrier_semaphore()
    for dr in range(nrow):
        for dc in range(ncol):
            if dr or dc:
                pl.semaphore_signal(
                    barrier, inc=1,
                    device_id={"row": (r + dr) % nrow, "col": (c + dc) % ncol},
                    device_id_type=MESH,
                )
    pl.semaphore_wait(barrier, nrow * ncol - 1)

    def rows(i):
        return pl.ds(pl.multiple_of(i * step, step), step)

    def y_copy(h, i):
        return remote(
            child_hbm.at[rows(i), halves[h]], gath.at[h, r, rows(i)],
            y_send.at[h, i], y_recv.at[h, i], across, c)

    def forward(h, i):
        spot = gath.at[h, across, rows(i)]
        return remote(spot, spot, f_send.at[h, i], f_recv.at[h, i], mate, c)

    def m_copy(h):
        return remote(
            child_hbm.at[:, halves[h]], gath.at[h, r], m_send.at[h], m_recv.at[h], mate, c)

    for i in range(nch):
        y_copy(0, i).start()
    for h in range(2):
        m_copy(h).start()

    def fac_copy(s, xd):
        return remote(
            fac_hbm.at[s], fac.at[core, c], fac_send.at[s, xd], fac_recv.at[core, c],
            2 * y, 2 * (1 + s) + xd)

    def fac_self(s, xd):
        return (core == 0) & (c == 2 * (1 + s) + xd)

    for s in range(2):
        for xd in range(2):
            @pl.when((c < r + nrow * s) & jnp.logical_not(fac_self(s, xd)))
            def _():
                fac_copy(s, xd).start()

            @pl.when((c < r + nrow * s) & fac_self(s, xd))
            def _():
                pltpu.make_async_copy(fac_hbm.at[s], fac.at[core, c], fac_recv.at[core, c]).start()

    def d_copy(xd):
        return remote(
            dinv_hbm.at[0], diag.at[x], d_send.at[xd], d_recv.at[x], r, 2 * (1 + z // 2) + xd)

    def r_copy(xd):
        return remote(
            rhs_hbm.at[0, :, pl.ds(xd * half, half)], rside.at[x], r_send.at[xd], r_recv.at[x],
            r, 2 * (1 + z // 2) + xd)

    def d_self(xd):
        return (z == 1 + z // 2) & (x == xd)

    for xd in range(2):
        @pl.when(home & jnp.logical_not(d_self(xd)))
        def _():
            d_copy(xd).start()
            r_copy(xd).start()

        @pl.when(home & d_self(xd))
        def _():
            pltpu.make_async_copy(dinv_hbm.at[0], diag.at[x], d_recv.at[x]).start()
            pltpu.make_async_copy(
                rhs_hbm.at[0, :, pl.ds(xd * half, half)], rside.at[x], r_recv.at[x]).start()

    acc[...] = jnp.zeros_like(acc)

    def piece(h, slot, i):
        cols = pl.ds(pl.multiple_of(slot * depth + i * step, step), step)
        block = gath[h, slot, rows(i)]
        for b in range(2):
            acc[h, b] += dot(cpl[b, :, cols], block)

    def flag(p, k):
        return jnp.where(pat_ref[2 * slab + p, k] > 0, 1.0, 0.0).astype(F32)

    def prepare():
        for p in range(2):
            arrival(diag.at[p], d_recv.at[p]).wait_recv()
            arrival(rside.at[p], r_recv.at[p]).wait_recv()
        for p in range(2):
            for k in range(ncol - 1):
                @pl.when(k < 2 * slab + p)
                def _():
                    arrival(fac.at[p, k], fac_recv.at[p, k]).wait_recv()
        inner = flag(1, 2 * slab) * dot(fac[1, 2 * slab], diag[0])
        below[...] = -dot(diag[1], inner.astype(BF16)).astype(BF16)
        for zz in range(nslab - 1):
            @pl.when(zz < slab)
            def _():
                @pl.loop(0, 2)
                def _(q):
                    k = 2 * zz + q
                    gain[zz, q, 0] = (flag(0, k) * dot(diag[0], fac[0, k])).astype(BF16)
                    gain[zz, q, 1] = (
                        flag(1, k) * dot(diag[1], fac[1, k]) + flag(0, k) * dot(below[...], fac[0, k])
                    ).astype(BF16)

    flags.wait()
    load.wait()
    for h in range(2):
        own[h].wait()

        @pl.loop(0, nch)
        def _(i):
            piece(h, r, i)

        arrival(gath.at[h, mate], m_recv.at[h]).wait_recv()

        @pl.loop(0, nch)
        def _(i):
            piece(h, mate, i)

        if h == 1:
            continue

        @pl.loop(0, nch)
        def _(i):
            arrival(gath.at[0, across, rows(i)], y_recv.at[0, i]).wait_recv()
            y_copy(1, i).start()
            forward(0, i).start()
            piece(0, across, i)
            arrival(gath.at[0, mate_across, rows(i)], f_recv.at[0, i]).wait_recv()
            piece(0, mate_across, i)

        xpart[...] = acc[0].astype(BF16)
        x_copy = remote(xpart, xrecv, x_sem.at[0], x_sem.at[1], r, beside)
        x_copy.start()
        pl.when(solver)(prepare)

    @pl.loop(0, nch)
    def _(i):
        arrival(gath.at[1, across, rows(i)], y_recv.at[1, i]).wait_recv()
        forward(1, i).start()
        piece(1, across, i)
        arrival(gath.at[1, mate_across, rows(i)], f_recv.at[1, i]).wait_recv()
        piece(1, mate_across, i)

    x_copy.wait_recv()

    def p_copy(s):
        return remote(
            part.at[s], precv.at[core, z], p_send.at[s], p_recv.at[core, z],
            2 * y, 2 * (1 + s) + x)

    def p_self(s):
        return solver & (z == 1 + s)

    for s in range(2):
        acc[1, s] = acc[1, s] + xrecv[s].astype(F32)
        part[s] = acc[1, s].astype(BF16)

        @pl.when(jnp.logical_not(p_self(s)))
        def _():
            p_copy(s).start()

    def chain_copy(zd):
        return remote(
            sol.at[slab], sol.at[slab], ch_send.at[zd], ch_recv.at[slab],
            2 * (zd % 2), 2 * (1 + zd // 2) + x)

    def out_copy(xo, ro):
        return remote(
            sol.at[slab, xo], out_ref.at[0, :, my_cols], o_send.at[xo, ro], o_recv.at[x],
            ro, 2 * slab + xo)

    def out_self(xo, ro):
        return (r == ro) & (slab == z) & (x == xo)

    def send_out(xo):
        for ro in range(0, nrow, 2):
            @pl.when(jnp.logical_not(out_self(xo, ro)))
            def _():
                out_copy(xo, ro).start()

    @pl.when(solver)
    def _():
        rest[0] = rside[0] - acc[1, z - 1]
        rest[1] = rside[1]
        for p in range(2):
            for k in range(nslab):
                def take():
                    arrival(precv.at[p, k], p_recv.at[p, k]).wait_recv()
                    rest[p] = rest[p] - precv[p, k].astype(F32)

                if p == 0:
                    pl.when(z != k)(take)
                else:
                    take()

        upper = rest[0].astype(BF16)
        lower = rest[1].astype(BF16)
        rest[0] = dot(diag[0], upper)
        rest[1] = dot(diag[1], lower) + dot(below[...], upper)
        for zz in range(nslab - 1):
            @pl.when(zz < slab)
            def _():
                arrival(sol.at[zz], ch_recv.at[zz]).wait_recv()
                for p in range(2):
                    rest[p] = rest[p] - (dot(gain[zz, 0, p], sol[zz, 0]) + dot(gain[zz, 1, p], sol[zz, 1]))

        sol[slab] = rest[...].astype(BF16)
        for zd in range(1, nslab):
            @pl.when(zd == slab + 1)
            def _():
                chain_copy(zd).start()
                chain_copy(zd).wait_send()
        for zd in range(2, nslab):
            @pl.when(zd > slab + 1)
            def _():
                chain_copy(zd).start()
        send_out(0)
        send_out(1)

        @pl.when(slab == z)
        def _():
            out_ref[0, :, my_cols] = sol[slab, x]

    def relay(xs):
        spot = out_ref.at[0, :, pl.ds(xs * half, half)]
        return remote(spot, spot, g_send.at[xs], o_recv.at[xs], mate, c)

    for xs in range(2):
        @pl.when(jnp.logical_not(solver & (slab == z) & (x == xs)))
        def _():
            arrival(out_ref.at[0, :, pl.ds(xs * half, half)], o_recv.at[xs]).wait_recv()

        @pl.when(core == 0)
        def _():
            relay(xs).start()

    m_copy(0).wait_send()
    m_copy(1).wait_send()
    x_copy.wait_send()
    for h in range(2):
        @pl.loop(0, nch)
        def _(i):
            y_copy(h, i).wait_send()
            forward(h, i).wait_send()

    for s in range(2):
        for xd in range(2):
            @pl.when((c < r + nrow * s) & jnp.logical_not(fac_self(s, xd)))
            def _():
                fac_copy(s, xd).wait_send()

            @pl.when((s == 0) & home & jnp.logical_not(d_self(xd)))
            def _():
                d_copy(xd).wait_send()
                r_copy(xd).wait_send()

        @pl.when(jnp.logical_not(p_self(s)))
        def _():
            p_copy(s).wait_send()

    @pl.when(core == 0)
    def _():
        for xs in range(2):
            relay(xs).wait_send()

    @pl.when(solver)
    def _():
        for zd in range(2, nslab):
            @pl.when(zd > slab + 1)
            def _():
                chain_copy(zd).wait_send()
        for xo in range(2):
            for ro in range(0, nrow, 2):
                @pl.when(jnp.logical_not(out_self(xo, ro)))
                def _():
                    out_copy(xo, ro).wait_send()


def fused(right_side, coupling, child_solution, factor_blocks, pattern, diag_inverse):
    nrow = lax.axis_size("row")
    ncol = lax.axis_size("col")
    brows, _, bs, kcols = coupling.shape
    depth, rhs = child_solution.shape
    nch = depth // 512
    half = rhs // 2
    dma = pltpu.SemaphoreType.DMA
    hbm = pl.BlockSpec(memory_space=pltpu.HBM)
    vmem = pl.BlockSpec(memory_space=pltpu.VMEM)
    flops = 2 * brows * bs * kcols * rhs
    return pl.pallas_call(
        functools.partial(kernel, nch),
        out_shape=jax.ShapeDtypeStruct((1, bs, rhs), BF16),
        in_specs=[hbm] * 6,
        out_specs=vmem,
        scratch_shapes=[
            pltpu.SMEM(pattern.shape, pattern.dtype),
            pltpu.VMEM((brows, bs, kcols), BF16),
            pltpu.VMEM((2, nrow, depth, half), BF16),
            pltpu.VMEM((2, brows, bs, half), F32),
            pltpu.VMEM((2, ncol, bs, bs), BF16),
            pltpu.VMEM((brows, bs, half), BF16),
            pltpu.VMEM((brows, bs, half), BF16),
            pltpu.VMEM((brows, bs, half), BF16),
            pltpu.VMEM((2, ncol // 2, bs, half), BF16),
            pltpu.VMEM((2, bs, bs), BF16),
            pltpu.VMEM((2, bs, half), F32),
            pltpu.VMEM((bs, bs), BF16),
            pltpu.VMEM((ncol // 2 - 1, 2, 2, bs, bs), BF16),
            pltpu.VMEM((2, bs, half), F32),
            pltpu.VMEM((ncol // 2, 2, bs, half), BF16),
            dma((4,)), dma((2,)), dma((2,)),
            dma((2, nch)), dma((2, nch)), dma((2, nch)), dma((2, nch)),
            dma((2, 2)), dma((2, ncol)), dma((2,)), dma((2,)), dma((2,)), dma((2,)), dma((2,)), dma((2,)), dma((2, ncol // 2)),
            dma((ncol // 2,)), dma((ncol // 2,)), dma((2, nrow)), dma((2,)), dma((2,)),
        ],
        compiler_params=pltpu.CompilerParams(
            collective_id=0, has_side_effects=True, vmem_limit_bytes=62 * 1024 * 1024
        ),
        cost_estimate=pl.CostEstimate(
            flops=flops, bytes_accessed=2 * brows * bs * kcols, transcendentals=0),
    )(
        right_side,
        coupling.reshape(brows, bs, kcols),
        child_solution,
        factor_blocks.reshape(brows, bs, bs),
        pattern,
        diag_inverse,
    )


def general(right_side, coupling, child_solution, factor_blocks, pattern, diag_inverse):
    nrow = lax.axis_size("row")
    ncol = lax.axis_size("col")
    row_index = lax.axis_index("row")
    col_index = lax.axis_index("col")
    brows = coupling.shape[0]
    blk_size = coupling.shape[2]
    kcols = coupling.shape[3]
    rhs_count = child_solution.shape[1]
    nblk = pattern.shape[0]
    group = ncol // nblk
    part_rows = blk_size // group
    my_block = col_index // group
    my_offset = col_index % group * part_rows
    flat = coupling.reshape(brows * blk_size, kcols)
    update = jnp.dot(
        flat,
        lax.all_gather(child_solution, "row", axis=0, tiled=True),
        preferred_element_type=jnp.float32,
    )
    update = update.reshape(brows, blk_size, rhs_count)
    rhs_part = right_side.reshape(part_rows, rhs_count)
    placed = lax.dynamic_update_slice(
        jnp.zeros((blk_size, rhs_count), jnp.float32), rhs_part, (my_offset, jnp.int32(0))
    )
    blocks = factor_blocks.reshape(brows, blk_size, part_rows)
    inv_rows = diag_inverse.reshape(part_rows, blk_size)

    def advance(j, solved):
        j_row = j % nrow
        j_arow = j // nrow
        flags = lax.dynamic_index_in_dim(pattern, j, 0, keepdims=False)
        flag = lax.dynamic_index_in_dim(flags, my_block, 0, keepdims=False)
        keep = (flag > 0) & (my_block < j)
        masked = jnp.where(keep, solved, jnp.zeros_like(solved))
        row_blocks = lax.dynamic_index_in_dim(blocks, j_arow, 0, keepdims=False)
        partial_value = jnp.dot(row_blocks, masked, preferred_element_type=jnp.float32)
        partial_value = partial_value + lax.dynamic_index_in_dim(update, j_arow, 0, keepdims=False)
        partial_value = jnp.where(my_block == j, placed, jnp.zeros_like(placed)) - partial_value
        partial_value = jnp.where(row_index == j_row, partial_value, jnp.zeros_like(partial_value))
        total = lax.psum(partial_value, ("col", "row"))
        fresh = jnp.dot(
            inv_rows, total.astype(jnp.bfloat16), preferred_element_type=jnp.float32
        ).astype(jnp.bfloat16)
        return jnp.where(my_block == j, fresh, solved)

    start_state = jnp.zeros((part_rows, rhs_count), jnp.bfloat16)
    solved = lax.fori_loop(0, nblk, advance, start_state)
    return solved.reshape(1, part_rows, rhs_count)


def solution(mesh):
    nrow, ncol = mesh.shape["row"], mesh.shape["col"]
    in_specs = (
        P("col", None, None),
        P(None, "row", None, "col"),
        P(("col", "row"), None),
        P(None, "row", None, "col", None),
        P(),
        P("col", None, None),
    )

    def per_device(right_side, coupling, child_solution, factor_blocks, pattern, diag_inverse):
        paired = nrow == 4 and ncol == 8 and pattern.shape[0] == 8
        body = fused if paired else general
        return body(right_side, coupling, child_solution, factor_blocks, pattern, diag_inverse)

    return jax.shard_map(
        per_device, mesh=mesh, in_specs=in_specs, out_specs=P("col", None, None), check_vma=False
    )
```
